32 devices in a mesh: groups: 2 (over y), grid: 4 (over z), layer: 4 (over x, core).
Axes of the slice: x: 2, y: 2, z: 4, core: 2. Of those that a mesh axis runs over, the one named last changes fastest.
Arguments:
- blocks: bfloat16 [64, 4, 128, 128], P(('groups', 'grid', 'layer')), parts along dimension 0, may hold values from -5 to 5
- columns: int32 [64, 4], P('groups'), parts along dimension 0, may hold values from 0 to 31, as said below
Outputs:
- sign_iterate: bfloat16 [64, 4, 128, 128], P(('groups', 'grid', 'layer')), parts along dimension 0
The draws below stay inside these ranges and needn't reach their ends.
There are 2 independent parts, one for each index of `groups`. The reference program is written for one: setup_inputs(seed, part) draws one part's arguments, and reference() takes and returns one part's arrays. A program takes and returns all parts, laid end to end along the dimension named above; each array names one. Nothing has to cross between parts.
Inputs may be any that keep to these rules, and one draw needn't show every extreme that they name: Slot 0 of block row i holds i. The other kept columns of a row are distinct block rows of panels whose grid index differs from the row's by exactly 1 cyclically, never rows of the same device; panel h holds block rows h * 8 to (h + 1) * 8 - 1. For each device and each of the 2 signed distances, at most 4 kept columns of its block rows lie at that distance, and exactly 4 for some device and distance.
All inputs are finite; a program needn't handle non-finite values.
Results may differ from the reference program's by a relative error of at most 0.0056.
Values may be sent and summed in bfloat16 or wider, within the bound.
A program may use at most 64 MiB of HBM per device.

```python
import jax
import jax.numpy as jnp
from jax import lax

BLOCK = 128
SLOTS = 4
ROWS_OWN = 2
STEPS = 2
REACH = 1
PANEL = 8
NB = 32
N_GRID = 4
N_LAYER = 4


def draw_columns(key, part):
    key = jax.random.fold_in(key, 7)
    moved_slots = ROWS_OWN * (SLOTS - 1)
    spare_rows = PANEL - ROWS_OWN
    dist_count = 2 * REACH
    key_shift, key_order = jax.random.split(key)
    offsets = jax.random.randint(key_shift, (N_GRID, N_LAYER, 1), 0, dist_count).astype(jnp.int32)
    order_keys = jax.random.split(key_order, N_GRID * N_LAYER)
    orders = jax.vmap(lambda single_key: jax.random.permutation(single_key, spare_rows))(order_keys)
    orders = orders.reshape(N_GRID, N_LAYER, spare_rows)[:, :, :moved_slots].astype(jnp.int32)
    slot_index = jnp.arange(moved_slots, dtype=jnp.int32)
    bucket = (offsets + slot_index[None, None, :] // 2) % dist_count
    shift_list = [step_one + 1 for step_one in range(REACH)] + [-(step_one + 1) for step_one in range(REACH)]
    step_table = jnp.array(shift_list, dtype=jnp.int32)
    signed_steps = step_table[bucket]
    grid_ids = jnp.arange(N_GRID, dtype=jnp.int32)[:, None, None]
    layer_ids = jnp.arange(N_LAYER, dtype=jnp.int32)[None, :, None]
    local_row = (layer_ids * ROWS_OWN + ROWS_OWN + orders) % PANEL
    remote_cols = (grid_ids + signed_steps) % N_GRID * PANEL + local_row
    remote_cols = remote_cols.reshape(N_GRID, N_LAYER, ROWS_OWN, SLOTS - 1)
    diagonal = grid_ids * PANEL + layer_ids * ROWS_OWN + jnp.arange(ROWS_OWN, dtype=jnp.int32)[None, None, :]
    columns = jnp.concatenate([diagonal[..., None], remote_cols], axis=-1).reshape(NB, SLOTS)
    return columns.astype(jnp.int32)


def levels(stream_key, shape, pieces, smallest, largest):
    level = 1.0
    for position, parts in pieces:
        steps = jax.random.uniform(jax.random.fold_in(jax.random.fold_in(stream_key, 6), position), (parts,), jnp.float32, smallest / len(pieces), largest / len(pieces))
        level = level * jnp.repeat(jnp.exp(steps), shape[position] // parts).reshape((-1,) + (1,) * (len(shape) - 1 - position))
    return level


def centred(key, dims, width, reach, shards=(), kind=jnp.bfloat16):
    result = width * jax.random.normal(key, dims, jnp.float32)
    if shards:
        result = result * levels(key, dims, shards, -0.22, 0.18)
    return jnp.clip(result, -reach, reach).astype(kind)


def setup_inputs(seed: int = 0, part: int = 0) -> dict:
    key_list = jax.random.split(jax.random.key(seed), 3)
    part_splits = jax.random.split(jax.random.fold_in(key_list[2], part), 3)
    return {
        "blocks": centred(part_splits[0], (NB, SLOTS, BLOCK, BLOCK), 0.8, 5.0, ((0, 16),)),
        "columns": draw_columns(jax.random.fold_in(jax.random.fold_in(key_list[2], part), 71), part),
    }


def pattern_product(multiplier, operand, columns):
    factor = (2.0 * BLOCK) ** -0.5

    def one_row(row_index):
        own_cols = columns[row_index]
        picked = operand[own_cols].astype(jnp.float32)
        picked_cols = columns[own_cols]
        partial_value = jnp.einsum("tij,tujk->tuik", multiplier[row_index].astype(jnp.float32), picked, precision=lax.Precision.HIGHEST)
        agree = (picked_cols[:, :, None] == own_cols[None, None, :]).astype(jnp.float32)
        return jnp.einsum("tus,tuik->sik", agree, partial_value, precision=lax.Precision.HIGHEST) * factor

    return lax.map(one_row, jnp.arange(NB, dtype=jnp.int32))


def reference(blocks, columns):
    current = blocks
    for turn in range(STEPS):
        square = pattern_product(current, current, columns).astype(jnp.bfloat16)
        cube = pattern_product(current, square, columns)
        current = (1.5 * current.astype(jnp.float32) - 0.5 * cube).astype(jnp.bfloat16)
    return current
```

```python
import functools

import jax
import jax.numpy as jnp
from jax import lax
from jax.experimental import pallas as pl
from jax.experimental.pallas import tpu as pltpu
from jax.sharding import PartitionSpec as P

STEPS = 2


def from_behind(block, axis, distance):
    devices = range(lax.axis_size(axis))
    route = [((i - distance) % len(devices), i) for i in devices]
    return lax.ppermute(block, axis, route)


def pattern_product(multiplier, operand, context):
    (
        own_cols,
        own_global,
        send_list,
        send_valid,
        columns,
        grid_pos,
        grid_size,
        panel_len,
        distances,
    ) = context
    rows_own = multiplier.shape[0]
    slots = multiplier.shape[1]
    width = multiplier.shape[2]
    flat_list = send_list.reshape(-1)
    flat_valid = send_valid.reshape(-1)
    piece = lax.all_gather(operand, "layer", axis=0, tiled=True)
    picker = (
        (flat_list[:, None] == jnp.arange(piece.shape[0])[None, :]) & flat_valid[:, None]
    ).astype(jnp.bfloat16)
    chosen = jnp.einsum("rn,nuij->ruij", picker, piece, preferred_element_type=jnp.float32)
    packed = chosen.astype(jnp.bfloat16)
    packed = packed.reshape(send_list.shape + (slots, width, width))
    arrived = []
    for kind in range(len(distances)):
        arrived.append(from_behind((packed[kind], send_list[kind]), "grid", -distances[kind]))
    cand_blocks = jnp.concatenate([operand] + [entry[0] for entry in arrived], axis=0)
    cand_parts = [own_global]
    for kind in range(len(distances)):
        source = (grid_pos + distances[kind]) % grid_size
        cand_parts.append(source * panel_len + arrived[kind][1])
    cand_rows = jnp.concatenate(cand_parts, axis=0).astype(jnp.int32)
    cand_cols = jnp.take(columns, cand_rows, axis=0)
    wanted = own_cols.reshape(-1)
    matches = wanted[:, None] == cand_rows[None, :]
    gathered = jnp.einsum(
        "ac,cuij->auij",
        matches.astype(jnp.bfloat16),
        cand_blocks,
        preferred_element_type=jnp.float32,
    ).astype(jnp.bfloat16)
    gathered_cols = jnp.max(jnp.where(matches[:, :, None], cand_cols[None, :, :], -1), axis=1)
    partial_value = jnp.einsum(
        "aij,aujk->auik",
        multiplier.reshape(-1, width, width),
        gathered,
        preferred_element_type=jnp.float32,
    )
    agree = (
        gathered_cols.reshape(rows_own, slots, slots)[:, :, :, None] == own_cols[:, None, None, :]
    ).astype(jnp.float32)
    summed = jnp.einsum(
        "qtus,qtuik->qsik",
        agree,
        partial_value.reshape(rows_own, slots, slots, width, width),
        precision=lax.Precision.HIGHEST,
    )
    return summed * (2.0 * width) ** (-0.5)


def local(blocks, columns):
    rows_own = blocks.shape[0]
    slots = blocks.shape[1]
    grid_size = lax.axis_size("grid")
    layer_size = lax.axis_size("layer")
    panel_len = rows_own * layer_size
    grid_pos = lax.axis_index("grid")
    layer_pos = lax.axis_index("layer")
    first_row = (grid_pos * layer_size + layer_pos) * rows_own
    own_global = first_row + jnp.arange(rows_own)
    own_cols = lax.dynamic_slice_in_dim(columns, first_row, rows_own, 0)
    reach = min(3, (grid_size - 1) // 2)
    moved_slots = rows_own * (slots - 1)
    pack_len = 2 * ((moved_slots + 4 * reach - 1) // (4 * reach))
    distances = [offset + 1 for offset in range(reach)] + [-(offset + 1) for offset in range(reach)]
    slot_index = jnp.arange(moved_slots, dtype=jnp.int32)
    position = jnp.arange(pack_len, dtype=jnp.int32)
    list_parts = []
    valid_parts = []
    for shift_by in distances:
        source_grid = (grid_pos - shift_by) % grid_size
        source_start = (source_grid * layer_size + layer_pos) * rows_own
        source_cols = lax.dynamic_slice_in_dim(columns, source_start, rows_own, 0)[:, 1:].reshape(
            -1
        )
        matched = source_cols // panel_len == grid_pos
        ordering = jnp.argsort(jnp.where(matched, 0, moved_slots) + slot_index)[:pack_len]
        local_rows = source_cols[ordering] - grid_pos * panel_len
        counted = jnp.sum(matched.astype(jnp.int32))
        valid_now = position < counted
        list_parts.append(jnp.where(valid_now, local_rows, 0))
        valid_parts.append(valid_now)
    send_list = jnp.stack(list_parts, axis=0)
    send_valid = jnp.stack(valid_parts, axis=0)
    context = (
        own_cols,
        own_global,
        send_list,
        send_valid,
        columns,
        grid_pos,
        grid_size,
        panel_len,
        distances,
    )
    current = blocks
    for turn in range(STEPS):
        square = pattern_product(current, current, context).astype(jnp.bfloat16)
        cube = pattern_product(current, square, context)
        current = (1.5 * current.astype(jnp.float32) - 0.5 * cube).astype(jnp.bfloat16)
    return current


GRID = 4
LAYER = 4
MESH = pl.DeviceIdType.MESH


class Exchange:
    def __init__(self, held, count, chunk, send, recv, place):
        self.held, self.count, self.chunk = held, count, chunk
        self.send, self.recv, self.place = send, recv, place
        self.started = []

    def part(self, side, layer, piece):
        start = (side * LAYER + layer) * self.count + piece * self.chunk
        return self.held.at[pl.ds(start, self.chunk)]

    def copy(self, source, stage, side, layer, piece, target):
        return pltpu.make_async_remote_copy(
            src_ref=source,
            dst_ref=self.part(side, layer, piece),
            send_sem=self.send.at[stage, side, piece],
            recv_sem=self.recv.at[stage, side, piece],
            device_id=target,
            device_id_type=MESH,
        )

    def start(self, source, stage, side, layer, piece, target):
        copy = self.copy(source, stage, side, layer, piece, target)
        copy.start()
        self.started.append(copy)

    def arrive(self, stage, side, layer, piece):
        part = self.part(side, layer, piece)
        self.copy(part, stage, side, layer, piece, {"layer": self.place.sibling}).wait_recv()

    def pieces(self):
        for piece in range(self.count // self.chunk):
            for side in range(2):
                yield side, piece

    def begin(self, source):
        at = self.place
        for side, piece in self.pieces():
            self.start(source(side, piece), 0, 1 - side, at.layer, piece, {"grid": at.panels[side]})

    def spread(self):
        at = self.place
        for side, piece in self.pieces():
            self.arrive(0, side, at.layer, piece)
            part = self.part(side, at.layer, piece)
            self.start(part, 2, side, at.layer, piece, {"layer": at.across})
            self.start(part, 1, side, at.layer, piece, {"layer": at.sibling})

    def relay(self):
        at = self.place
        for side, piece in self.pieces():
            self.arrive(2, side, at.across, piece)
            part = self.part(side, at.across, piece)
            self.start(part, 3, side, at.across, piece, {"layer": at.sibling})

    def finish(self):
        at = self.place
        for side, piece in self.pieces():
            self.arrive(1, side, at.sibling, piece)
            self.arrive(3, side, at.opposite, piece)

    def drain(self):
        for copy in self.started:
            copy.wait_send()


class Place:
    def __init__(self):
        self.grid = lax.axis_index("grid")
        self.layer = lax.axis_index("layer")
        self.panels = (
            lax.rem(self.grid + 1, GRID),
            lax.rem(self.grid + GRID - 1, GRID),
        )
        self.sibling = self.layer + 1 - 2 * lax.rem(self.layer, 2)
        self.across = lax.rem(self.layer + 2, LAYER)
        self.opposite = lax.rem(self.sibling + 2, LAYER)


def dot(left, right):
    return jnp.dot(left, right, preferred_element_type=jnp.float32)


def kernel(
    rows,
    slots,
    cap,
    cols,
    x,
    out,
    pack,
    mutual,
    diag,
    sq_diag,
    diag1,
    sq_diag1,
    own_sq,
    own_diag1,
    own_sq1,
    sq,
    sq_mut,
    x1,
    x1_mut,
    send_m,
    recv_m,
    send_d,
    recv_d,
):
    place = Place()
    panel = rows * LAYER
    first = (place.grid * LAYER + place.layer) * rows
    width = x.shape[-1]
    factor = (2.0 * width) ** (-0.5)
    kept = [(a, t) for a in range(rows) for t in range(1, slots)]

    barrier = pltpu.get_barrier_semaphore()
    for target in (
        {"grid": place.panels[0]},
        {"grid": place.panels[1]},
        {"layer": place.sibling},
        {"layer": place.across},
    ):
        pl.semaphore_signal(barrier, inc=1, device_id=target, device_id_type=MESH)

    own_cols = {(a, t): cols[first + a, t] for a, t in kept}
    ahead = {
        key: ((col // panel) == place.panels[0]).astype(jnp.int32) for key, col in own_cols.items()
    }
    for side in range(2):
        source_row = [jnp.int32(0)] * cap
        source_slot = [jnp.int32(1)] * cap
        rank = jnp.int32(0)
        for a, t in kept:
            here = ahead[a, t] if side == 0 else 1 - ahead[a, t]
            for k in range(cap):
                taken = (here == 1) & (rank == k)
                source_row[k] = jnp.where(taken, a, source_row[k])
                source_slot[k] = jnp.where(taken, t, source_slot[k])
            rank = rank + here
        for k in range(cap):
            pack[side, k] = x[source_row[k], source_slot[k]]
    nothing = 2 * LAYER * cap
    mutual[nothing] = jnp.zeros((width, width), jnp.bfloat16)

    pl.semaphore_wait(barrier, 4)

    def trade(held, which):
        return Exchange(held, rows, 1, send_d.at[which], recv_d.at[which], place)

    m_trade = Exchange(mutual, cap, MUTUAL_CHUNK, send_m, recv_m, place)
    d_trade, s_trade, d1_trade, s1_trade = [
        trade(held, which) for which, held in enumerate((diag, sq_diag, diag1, sq_diag1))
    ]
    m_trade.begin(lambda side, piece: pack.at[side, pl.ds(piece * MUTUAL_CHUNK, MUTUAL_CHUNK)])
    d_trade.begin(lambda side, piece: x.at[piece, pl.ds(0, 1)])

    at_diag = {}
    at_mutual = {}
    for a, t in kept:
        col = own_cols[a, t]
        side = 1 - ahead[a, t]
        inner = lax.rem(col, panel)
        owner = inner // rows
        within = lax.rem(inner, rows)
        start = col - within
        at_diag[a, t] = (side * LAYER + owner) * rows + within
        found = jnp.int32(nothing)
        rank = jnp.int32(0)
        for b, u in kept:
            theirs = cols[start + b, u]
            hit = (within == b) & (theirs == first + a)
            found = jnp.where(hit, (side * LAYER + owner) * cap + rank, found)
            rank = rank + (theirs // panel == place.grid).astype(jnp.int32)
        at_mutual[a, t] = found

    def row_dot(left, right):
        return dot(jnp.concatenate(left, axis=1), jnp.concatenate(right, axis=0))

    def rounded(product):
        return (product * factor).astype(jnp.bfloat16)

    def stepped(old, product):
        return (1.5 * old.astype(jnp.float32) - 0.5 * (product * factor)).astype(jnp.bfloat16)

    m_trade.spread()
    d_trade.spread()
    m_trade.relay()
    m_trade.finish()

    for a in range(rows):
        met = [x[a, 0]] + [mutual[at_mutual[a, t]] for t in range(1, slots)]
        own_sq[a] = rounded(row_dot([x[a, t] for t in range(slots)], met))
    s_trade.begin(lambda side, piece: own_sq.at[pl.ds(piece, 1)])

    d_trade.relay()
    d_trade.finish()

    for a, t in kept:
        theirs, theirs_diag = mutual[at_mutual[a, t]], diag[at_diag[a, t]]
        sq_mut[a, t - 1] = rounded(row_dot([theirs_diag, theirs], [theirs, x[a, 0]]))
    for a in range(rows):
        met = [own_sq[a]] + [sq_mut[a, t - 1] for t in range(1, slots)]
        own_diag1[a] = stepped(x[a, 0], row_dot([x[a, t] for t in range(slots)], met))
    d1_trade.begin(lambda side, piece: own_diag1.at[pl.ds(piece, 1)])

    s_trade.spread()
    for a, t in kept:
        sq[a, t - 1] = rounded(row_dot([x[a, 0], x[a, t]], [x[a, t], diag[at_diag[a, t]]]))
    s_trade.relay()
    for a, t in kept:
        theirs, theirs_diag = mutual[at_mutual[a, t]], diag[at_diag[a, t]]
        x1_mut[a, t - 1] = stepped(
            theirs, row_dot([theirs_diag, theirs], [sq_mut[a, t - 1], own_sq[a]])
        )
    s_trade.finish()

    for a, t in kept:
        x1[a, t - 1] = stepped(
            x[a, t], row_dot([x[a, 0], x[a, t]], [sq[a, t - 1], sq_diag[at_diag[a, t]]])
        )
    for a in range(rows):
        left = [own_diag1[a]] + [x1[a, t - 1] for t in range(1, slots)]
        right = [own_diag1[a]] + [x1_mut[a, t - 1] for t in range(1, slots)]
        own_sq1[a] = rounded(row_dot(left, right))
    s1_trade.begin(lambda side, piece: own_sq1.at[pl.ds(piece, 1)])

    d1_trade.spread()
    d1_trade.relay()
    d1_trade.finish()
    s1_trade.spread()

    for a, t in kept:
        theirs, theirs_diag = x1_mut[a, t - 1], diag1[at_diag[a, t]]
        sq_mut[a, t - 1] = rounded(row_dot([theirs_diag, theirs], [theirs, own_diag1[a]]))
        sq[a, t - 1] = rounded(
            row_dot([own_diag1[a], x1[a, t - 1]], [x1[a, t - 1], theirs_diag])
        )
    s1_trade.relay()
    for a in range(rows):
        left = [own_diag1[a]] + [x1[a, t - 1] for t in range(1, slots)]
        met = [own_sq1[a]] + [sq_mut[a, t - 1] for t in range(1, slots)]
        out[a, 0] = stepped(own_diag1[a], row_dot(left, met))
    s1_trade.finish()
    for a, t in kept:
        out[a, t] = stepped(
            x1[a, t - 1],
            row_dot([own_diag1[a], x1[a, t - 1]], [sq[a, t - 1], sq_diag1[at_diag[a, t]]]),
        )
    for each in (m_trade, d_trade, s_trade, d1_trade, s1_trade):
        each.drain()


MUTUAL_CHUNK = 2


def local_kernel(blocks, columns):
    rows, slots, width, _ = blocks.shape
    moved = rows * (slots - 1)
    cap = 2 * ((moved + 3) // 4)

    def held(*dims):
        return pltpu.VMEM(dims + (width, width), jnp.bfloat16)

    beside = 2 * LAYER * rows
    m_sems = (4, 2, cap // MUTUAL_CHUNK)
    d_sems = (4, 4, 2, rows)
    return pl.pallas_call(
        functools.partial(kernel, rows, slots, cap),
        out_shape=jax.ShapeDtypeStruct(blocks.shape, blocks.dtype),
        in_specs=[
            pl.BlockSpec(memory_space=pltpu.SMEM),
            pl.BlockSpec(memory_space=pltpu.VMEM),
        ],
        out_specs=pl.BlockSpec(memory_space=pltpu.VMEM),
        scratch_shapes=[
            held(2, cap),
            held(2 * LAYER * cap + 1),
            held(beside),
            held(beside),
            held(beside),
            held(beside),
            held(rows),
            held(rows),
            held(rows),
            held(rows, slots - 1),
            held(rows, slots - 1),
            held(rows, slots - 1),
            held(rows, slots - 1),
            pltpu.SemaphoreType.DMA(m_sems),
            pltpu.SemaphoreType.DMA(m_sems),
            pltpu.SemaphoreType.DMA(d_sems),
            pltpu.SemaphoreType.DMA(d_sems),
        ],
        compiler_params=pltpu.CompilerParams(
            collective_id=0, has_side_effects=True, vmem_limit_bytes=32 * 1024 * 1024
        ),
        name="sign_iterations",
    )(columns, blocks)


def solution(mesh):
    placed = (P(("groups", "grid", "layer"), None, None, None), P("groups", None))
    four_panels = mesh.shape["grid"] == GRID and mesh.shape["layer"] == LAYER
    return jax.shard_map(
        local_kernel if four_panels else local,
        mesh=mesh,
        in_specs=placed,
        out_specs=P(("groups", "grid", "layer"), None, None, None),
        check_vma=False,
    )
```

```python
import functools

import jax
import jax.numpy as jnp
from jax import lax
from jax.experimental import pallas as pl
from jax.experimental.pallas import tpu as pltpu
from jax.sharding import PartitionSpec as P

STEPS = 2


def from_behind(block, axis, distance):
    devices = range(lax.axis_size(axis))
    route = [((i - distance) % len(devices), i) for i in devices]
    return lax.ppermute(block, axis, route)


def pattern_product(multiplier, operand, context):
    (
        own_cols,
        own_global,
        send_list,
        send_valid,
        columns,
        grid_pos,
        grid_size,
        panel_len,
        distances,
    ) = context
    rows_own = multiplier.shape[0]
    slots = multiplier.shape[1]
    width = multiplier.shape[2]
    flat_list = send_list.reshape(-1)
    flat_valid = send_valid.reshape(-1)
    piece = lax.all_gather(operand, "layer", axis=0, tiled=True)
    picker = (
        (flat_list[:, None] == jnp.arange(piece.shape[0])[None, :]) & flat_valid[:, None]
    ).astype(jnp.bfloat16)
    chosen = jnp.einsum("rn,nuij->ruij", picker, piece, preferred_element_type=jnp.float32)
    packed = chosen.astype(jnp.bfloat16)
    packed = packed.reshape(send_list.shape + (slots, width, width))
    arrived = []
    for kind in range(len(distances)):
        arrived.append(from_behind((packed[kind], send_list[kind]), "grid", -distances[kind]))
    cand_blocks = jnp.concatenate([operand] + [entry[0] for entry in arrived], axis=0)
    cand_parts = [own_global]
    for kind in range(len(distances)):
        source = (grid_pos + distances[kind]) % grid_size
        cand_parts.append(source * panel_len + arrived[kind][1])
    cand_rows = jnp.concatenate(cand_parts, axis=0).astype(jnp.int32)
    cand_cols = jnp.take(columns, cand_rows, axis=0)
    wanted = own_cols.reshape(-1)
    matches = wanted[:, None] == cand_rows[None, :]
    gathered = jnp.einsum(
        "ac,cuij->auij",
        matches.astype(jnp.bfloat16),
        cand_blocks,
        preferred_element_type=jnp.float32,
    ).astype(jnp.bfloat16)
    gathered_cols = jnp.max(jnp.where(matches[:, :, None], cand_cols[None, :, :], -1), axis=1)
    partial_value = jnp.einsum(
        "aij,aujk->auik",
        multiplier.reshape(-1, width, width),
        gathered,
        preferred_element_type=jnp.float32,
    )
    agree = (
        gathered_cols.reshape(rows_own, slots, slots)[:, :, :, None] == own_cols[:, None, None, :]
    ).astype(jnp.float32)
    summed = jnp.einsum(
        "qtus,qtuik->qsik",
        agree,
        partial_value.reshape(rows_own, slots, slots, width, width),
        precision=lax.Precision.HIGHEST,
    )
    return summed * (2.0 * width) ** (-0.5)


def local(blocks, columns):
    rows_own = blocks.shape[0]
    slots = blocks.shape[1]
    grid_size = lax.axis_size("grid")
    layer_size = lax.axis_size("layer")
    panel_len = rows_own * layer_size
    grid_pos = lax.axis_index("grid")
    layer_pos = lax.axis_index("layer")
    first_row = (grid_pos * layer_size + layer_pos) * rows_own
    own_global = first_row + jnp.arange(rows_own)
    own_cols = lax.dynamic_slice_in_dim(columns, first_row, rows_own, 0)
    reach = min(3, (grid_size - 1) // 2)
    moved_slots = rows_own * (slots - 1)
    pack_len = 2 * ((moved_slots + 4 * reach - 1) // (4 * reach))
    distances = [offset + 1 for offset in range(reach)] + [-(offset + 1) for offset in range(reach)]
    slot_index = jnp.arange(moved_slots, dtype=jnp.int32)
    position = jnp.arange(pack_len, dtype=jnp.int32)
    list_parts = []
    valid_parts = []
    for shift_by in distances:
        source_grid = (grid_pos - shift_by) % grid_size
        source_start = (source_grid * layer_size + layer_pos) * rows_own
        source_cols = lax.dynamic_slice_in_dim(columns, source_start, rows_own, 0)[:, 1:].reshape(
            -1
        )
        matched = source_cols // panel_len == grid_pos
        ordering = jnp.argsort(jnp.where(matched, 0, moved_slots) + slot_index)[:pack_len]
        local_rows = source_cols[ordering] - grid_pos * panel_len
        counted = jnp.sum(matched.astype(jnp.int32))
        valid_now = position < counted
        list_parts.append(jnp.where(valid_now, local_rows, 0))
        valid_parts.append(valid_now)
    send_list = jnp.stack(list_parts, axis=0)
    send_valid = jnp.stack(valid_parts, axis=0)
    context = (
        own_cols,
        own_global,
        send_list,
        send_valid,
        columns,
        grid_pos,
        grid_size,
        panel_len,
        distances,
    )
    current = blocks
    for turn in range(STEPS):
        square = pattern_product(current, current, context).astype(jnp.bfloat16)
        cube = pattern_product(current, square, context)
        current = (1.5 * current.astype(jnp.float32) - 0.5 * cube).astype(jnp.bfloat16)
    return current


GRID = 4
LAYER = 4
MESH = pl.DeviceIdType.MESH


class Exchange:
    def __init__(self, held, ways, send, recv, place):
        self.held, self.ways, self.send, self.recv, self.place = held, ways, send, recv, place
        self.started = []

    def part(self, side, layer, piece):
        return self.held.at[pl.ds((side * LAYER + layer) * len(self.ways) + piece, 1)]

    def copy(self, source, stage, side, layer, piece, target):
        return pltpu.make_async_remote_copy(
            src_ref=source,
            dst_ref=self.part(side, layer, piece),
            send_sem=self.send.at[stage, side, piece],
            recv_sem=self.recv.at[stage, side, piece],
            device_id=target,
            device_id_type=MESH,
        )

    def start(self, source, stage, side, layer, piece, target):
        copy = self.copy(source, stage, side, layer, piece, target)
        copy.start()
        self.started.append(copy)

    def arrive(self, stage, side, layer, piece):
        part = self.part(side, layer, piece)
        self.copy(part, stage, side, layer, piece, {"layer": self.place.sibling}).wait_recv()

    def begin(self, source, pieces=None):
        at = self.place
        for piece in range(len(self.ways)) if pieces is None else pieces:
            for side in (at.far, 1 - at.far):
                panel, mine = at.panel(side), source(side, piece)
                self.start(mine, 0, 1 - side, at.layer, piece, {"grid": panel})
                if self.ways[piece] == "direct":
                    target = {"grid": panel, "layer": at.across}
                    self.start(mine, 2, 1 - side, at.layer, piece, target)

    def spread(self, pieces=None):
        at = self.place
        for piece in range(len(self.ways)) if pieces is None else pieces:
            for side in (1 - at.far, at.far):
                self.arrive(0, side, at.layer, piece)
                part = self.part(side, at.layer, piece)
                if self.ways[piece] != "direct":
                    self.start(part, 2, side, at.layer, piece, {"layer": at.across})
                if self.ways[piece] == "both":
                    self.start(part, 3, side, at.layer, piece, {"layer": at.opposite})
                self.start(part, 1, side, at.layer, piece, {"layer": at.sibling})

    def relay(self):
        at = self.place
        for piece, way in enumerate(self.ways):
            for side in (1 - at.far, at.far):
                if way != "both":
                    self.arrive(2, side, at.across, piece)
                    part = self.part(side, at.across, piece)
                    self.start(part, 3, side, at.across, piece, {"layer": at.sibling})

    def finish(self):
        at = self.place
        for piece, way in enumerate(self.ways):
            for side in (1 - at.far, at.far):
                if way == "both":
                    self.arrive(2, side, at.across, piece)
                self.arrive(1, side, at.sibling, piece)
                self.arrive(3, side, at.opposite, piece)

    def drain(self):
        for copy in self.started:
            copy.wait_send()


class Place:
    def __init__(self):
        self.grid = lax.axis_index("grid")
        self.layer = lax.axis_index("layer")
        self.sibling = self.layer + 1 - 2 * lax.rem(self.layer, 2)
        self.across = lax.rem(self.layer + 2, LAYER)
        self.opposite = lax.rem(self.sibling + 2, LAYER)
        self.far = 1 - self.grid // (GRID - 1)

    def panel(self, side):
        return lax.rem(self.grid + 1 + (GRID - 2) * side, GRID)


def calm(count):
    return ["relay"] * count


def urgent(count):
    return ["both"] * (count - 1) + ["direct"]


def mutual_ways(count):
    return ["relay"] * (count - 2) + ["both", "direct"]


def dot(left, right):
    return jnp.dot(left, right, preferred_element_type=jnp.float32)


def kernel(
    rows,
    slots,
    cap,
    cols_in,
    x_in,
    out,
    cols,
    x,
    pack,
    mutual,
    diag,
    sq_diag,
    diag1,
    sq_diag1,
    own_sq,
    own_diag1,
    own_sq1,
    sq,
    sq_mut,
    x1,
    x1_mut,
    send_m,
    recv_m,
    send_d,
    recv_d,
    load_sem,
):
    place = Place()
    panel = rows * LAYER
    first = (place.grid * LAYER + place.layer) * rows
    width = x.shape[-1]
    factor = (2.0 * width) ** (-0.5)
    kept = [(a, t) for a in range(rows) for t in range(1, slots)]

    barrier = pltpu.get_barrier_semaphore()
    before, after = {"grid": place.panel(1)}, {"grid": place.panel(0)}
    across = {"layer": place.across}
    partners = [before, after, before | across, after | across, across]
    partners += [{"layer": place.sibling}, {"layer": place.opposite}]
    for target in partners:
        pl.semaphore_signal(barrier, inc=1, device_id=target, device_id_type=MESH)
    loads = [
        pltpu.make_async_copy(cols_in, cols, load_sem.at[0]),
        pltpu.make_async_copy(x_in, x, load_sem.at[1]),
    ]
    for load in loads:
        load.start()
    for load in loads:
        load.wait()

    own_cols = {(a, t): cols[t, first + a] for a, t in kept}
    ahead = {
        key: ((col // panel) == place.panel(0)).astype(jnp.int32) for key, col in own_cols.items()
    }
    for side in range(2):
        source_row = [jnp.int32(0)] * cap
        source_slot = [jnp.int32(1)] * cap
        rank = jnp.int32(0)
        for a, t in kept:
            here = ahead[a, t] if side == 0 else 1 - ahead[a, t]
            for k in range(cap):
                taken = (here == 1) & (rank == k)
                source_row[k] = jnp.where(taken, a, source_row[k])
                source_slot[k] = jnp.where(taken, t, source_slot[k])
            rank = rank + here
        for k in range(cap):
            pack[side, k] = x[source_row[k], source_slot[k]]
    nothing = 2 * LAYER * cap
    mutual[nothing] = jnp.zeros((width, width), jnp.bfloat16)

    pl.semaphore_wait(barrier, len(partners))

    m_trade = Exchange(mutual, mutual_ways(cap), send_m, recv_m, place)
    d_trade, s_trade, d1_trade, s1_trade = [
        Exchange(held, ways(rows), send_d.at[which], recv_d.at[which], place)
        for which, (held, ways) in enumerate(
            ((diag, calm), (sq_diag, urgent), (diag1, calm), (sq_diag1, urgent))
        )
    ]
    m_trade.begin(lambda side, piece: pack.at[side, pl.ds(piece, 1)])
    d_trade.begin(lambda side, piece: x.at[piece, pl.ds(0, 1)])

    at_diag = {}
    at_mutual = {}
    for a, t in kept:
        col = own_cols[a, t]
        side = 1 - ahead[a, t]
        inner = lax.rem(col, panel)
        owner = inner // rows
        within = lax.rem(inner, rows)
        start = col - within
        at_diag[a, t] = (side * LAYER + owner) * rows + within
        found = jnp.int32(nothing)
        rank = jnp.int32(0)
        for b, u in kept:
            theirs = cols[u, start + b]
            hit = (within == b) & (theirs == first + a)
            found = jnp.where(hit, (side * LAYER + owner) * cap + rank, found)
            rank = rank + (theirs // panel == place.grid).astype(jnp.int32)
        at_mutual[a, t] = found

    def row_dot(left, right):
        return dot(jnp.concatenate(left, axis=1), jnp.concatenate(right, axis=0))

    def rounded(product):
        return (product * factor).astype(jnp.bfloat16)

    def stepped(old, product):
        return (1.5 * old.astype(jnp.float32) - 0.5 * (product * factor)).astype(jnp.bfloat16)

    m_trade.spread()
    m_trade.relay()
    m_trade.finish()

    for a in range(rows):
        met = [x[a, 0]] + [mutual[at_mutual[a, t]] for t in range(1, slots)]
        own_sq[a] = rounded(row_dot([x[a, t] for t in range(slots)], met))
    s_trade.begin(lambda side, piece: own_sq.at[pl.ds(piece, 1)])

    d_trade.spread()
    d_trade.relay()
    d_trade.finish()
    s_trade.spread([0])

    for a, t in kept:
        theirs, theirs_diag = mutual[at_mutual[a, t]], diag[at_diag[a, t]]
        sq_mut[a, t - 1] = rounded(row_dot([theirs_diag, theirs], [theirs, x[a, 0]]))
    for a in range(rows):
        met = [own_sq[a]] + [sq_mut[a, t - 1] for t in range(1, slots)]
        own_diag1[a] = stepped(x[a, 0], row_dot([x[a, t] for t in range(slots)], met))
    d1_trade.begin(lambda side, piece: own_diag1.at[pl.ds(piece, 1)])

    s_trade.spread(range(1, rows))
    for a, t in kept:
        sq[a, t - 1] = rounded(row_dot([x[a, 0], x[a, t]], [x[a, t], diag[at_diag[a, t]]]))
    s_trade.relay()
    for a, t in kept:
        theirs, theirs_diag = mutual[at_mutual[a, t]], diag[at_diag[a, t]]
        x1_mut[a, t - 1] = stepped(
            theirs, row_dot([theirs_diag, theirs], [sq_mut[a, t - 1], own_sq[a]])
        )
    s_trade.finish()

    for a, t in kept:
        x1[a, t - 1] = stepped(
            x[a, t], row_dot([x[a, 0], x[a, t]], [sq[a, t - 1], sq_diag[at_diag[a, t]]])
        )
    for a in range(rows):
        left = [own_diag1[a]] + [x1[a, t - 1] for t in range(1, slots)]
        right = [own_diag1[a]] + [x1_mut[a, t - 1] for t in range(1, slots)]
        own_sq1[a] = rounded(row_dot(left, right))
    s1_trade.begin(lambda side, piece: own_sq1.at[pl.ds(piece, 1)])

    d1_trade.spread()
    s1_trade.spread([0])
    d1_trade.relay()
    d1_trade.finish()

    for a, t in kept:
        theirs, theirs_diag = x1_mut[a, t - 1], diag1[at_diag[a, t]]
        sq_mut[a, t - 1] = rounded(row_dot([theirs_diag, theirs], [theirs, own_diag1[a]]))
        sq[a, t - 1] = rounded(
            row_dot([own_diag1[a], x1[a, t - 1]], [x1[a, t - 1], theirs_diag])
        )
    s1_trade.spread(range(1, rows))
    s1_trade.relay()
    for a in range(rows):
        left = [own_diag1[a]] + [x1[a, t - 1] for t in range(1, slots)]
        met = [own_sq1[a]] + [sq_mut[a, t - 1] for t in range(1, slots)]
        out[a, 0] = stepped(own_diag1[a], row_dot(left, met))
    s1_trade.finish()
    for a, t in kept:
        out[a, t] = stepped(
            x1[a, t - 1],
            row_dot([own_diag1[a], x1[a, t - 1]], [sq[a, t - 1], sq_diag1[at_diag[a, t]]]),
        )
    for each in (m_trade, d_trade, s_trade, d1_trade, s1_trade):
        each.drain()


def local_kernel(blocks, columns):
    rows, slots, width, _ = blocks.shape
    moved = rows * (slots - 1)
    cap = 2 * ((moved + 3) // 4)

    def held(*dims):
        return pltpu.VMEM(dims + (width, width), jnp.bfloat16)

    beside = 2 * LAYER * rows
    m_sems = (4, 2, cap)
    d_sems = (4, 4, 2, rows)
    return pl.pallas_call(
        functools.partial(kernel, rows, slots, cap),
        out_shape=jax.ShapeDtypeStruct(blocks.shape, blocks.dtype),
        in_specs=[
            pl.BlockSpec(memory_space=pltpu.HBM),
            pl.BlockSpec(memory_space=pltpu.HBM),
        ],
        out_specs=pl.BlockSpec(memory_space=pltpu.VMEM),
        scratch_shapes=[
            pltpu.SMEM(columns.shape[::-1], columns.dtype),
            pltpu.VMEM(blocks.shape, blocks.dtype),
            held(2, cap),
            held(2 * LAYER * cap + 1),
            held(beside),
            held(beside),
            held(beside),
            held(beside),
            held(rows),
            held(rows),
            held(rows),
            held(rows, slots - 1),
            held(rows, slots - 1),
            held(rows, slots - 1),
            held(rows, slots - 1),
            pltpu.SemaphoreType.DMA(m_sems),
            pltpu.SemaphoreType.DMA(m_sems),
            pltpu.SemaphoreType.DMA(d_sems),
            pltpu.SemaphoreType.DMA(d_sems),
            pltpu.SemaphoreType.DMA((2,)),
        ],
        compiler_params=pltpu.CompilerParams(
            collective_id=0, has_side_effects=True, vmem_limit_bytes=64 * 1024 * 1024
        ),
        name="sign_iterations",
    )(columns.T, blocks)


def solution(mesh):
    placed = (P(("groups", "grid", "layer"), None, None, None), P("groups", None))
    four_panels = mesh.shape["grid"] == GRID and mesh.shape["layer"] == LAYER
    return jax.shard_map(
        local_kernel if four_panels else local,
        mesh=mesh,
        in_specs=placed,
        out_specs=P(("groups", "grid", "layer"), None, None, None),
        check_vma=False,
    )
```

```python
import functools

import jax
import jax.numpy as jnp
from jax import lax
from jax.experimental import pallas as pl
from jax.experimental.pallas import tpu as pltpu
from jax.sharding import PartitionSpec as P

STEPS = 2


def from_behind(block, axis, distance):
    devices = range(lax.axis_size(axis))
    route = [((i - distance) % len(devices), i) for i in devices]
    return lax.ppermute(block, axis, route)


def pattern_product(multiplier, operand, context):
    (
        own_cols,
        own_global,
        send_list,
        send_valid,
        columns,
        grid_pos,
        grid_size,
        panel_len,
        distances,
    ) = context
    rows_own = multiplier.shape[0]
    slots = multiplier.shape[1]
    width = multiplier.shape[2]
    flat_list = send_list.reshape(-1)
    flat_valid = send_valid.reshape(-1)
    piece = lax.all_gather(operand, "layer", axis=0, tiled=True)
    picker = (
        (flat_list[:, None] == jnp.arange(piece.shape[0])[None, :]) & flat_valid[:, None]
    ).astype(jnp.bfloat16)
    chosen = jnp.einsum("rn,nuij->ruij", picker, piece, preferred_element_type=jnp.float32)
    packed = chosen.astype(jnp.bfloat16)
    packed = packed.reshape(send_list.shape + (slots, width, width))
    arrived = []
    for kind in range(len(distances)):
        arrived.append(from_behind((packed[kind], send_list[kind]), "grid", -distances[kind]))
    cand_blocks = jnp.concatenate([operand] + [entry[0] for entry in arrived], axis=0)
    cand_parts = [own_global]
    for kind in range(len(distances)):
        source = (grid_pos + distances[kind]) % grid_size
        cand_parts.append(source * panel_len + arrived[kind][1])
    cand_rows = jnp.concatenate(cand_parts, axis=0).astype(jnp.int32)
    cand_cols = jnp.take(columns, cand_rows, axis=0)
    wanted = own_cols.reshape(-1)
    matches = wanted[:, None] == cand_rows[None, :]
    gathered = jnp.einsum(
        "ac,cuij->auij",
        matches.astype(jnp.bfloat16),
        cand_blocks,
        preferred_element_type=jnp.float32,
    ).astype(jnp.bfloat16)
    gathered_cols = jnp.max(jnp.where(matches[:, :, None], cand_cols[None, :, :], -1), axis=1)
    partial_value = jnp.einsum(
        "aij,aujk->auik",
        multiplier.reshape(-1, width, width),
        gathered,
        preferred_element_type=jnp.float32,
    )
    agree = (
        gathered_cols.reshape(rows_own, slots, slots)[:, :, :, None] == own_cols[:, None, None, :]
    ).astype(jnp.float32)
    summed = jnp.einsum(
        "qtus,qtuik->qsik",
        agree,
        partial_value.reshape(rows_own, slots, slots, width, width),
        precision=lax.Precision.HIGHEST,
    )
    return summed * (2.0 * width) ** (-0.5)


def local(blocks, columns):
    rows_own = blocks.shape[0]
    slots = blocks.shape[1]
    grid_size = lax.axis_size("grid")
    layer_size = lax.axis_size("layer")
    panel_len = rows_own * layer_size
    grid_pos = lax.axis_index("grid")
    layer_pos = lax.axis_index("layer")
    first_row = (grid_pos * layer_size + layer_pos) * rows_own
    own_global = first_row + jnp.arange(rows_own)
    own_cols = lax.dynamic_slice_in_dim(columns, first_row, rows_own, 0)
    reach = min(3, (grid_size - 1) // 2)
    moved_slots = rows_own * (slots - 1)
    pack_len = 2 * ((moved_slots + 4 * reach - 1) // (4 * reach))
    distances = [offset + 1 for offset in range(reach)] + [-(offset + 1) for offset in range(reach)]
    slot_index = jnp.arange(moved_slots, dtype=jnp.int32)
    position = jnp.arange(pack_len, dtype=jnp.int32)
    list_parts = []
    valid_parts = []
    for shift_by in distances:
        source_grid = (grid_pos - shift_by) % grid_size
        source_start = (source_grid * layer_size + layer_pos) * rows_own
        source_cols = lax.dynamic_slice_in_dim(columns, source_start, rows_own, 0)[:, 1:].reshape(
            -1
        )
        matched = source_cols // panel_len == grid_pos
        ordering = jnp.argsort(jnp.where(matched, 0, moved_slots) + slot_index)[:pack_len]
        local_rows = source_cols[ordering] - grid_pos * panel_len
        counted = jnp.sum(matched.astype(jnp.int32))
        valid_now = position < counted
        list_parts.append(jnp.where(valid_now, local_rows, 0))
        valid_parts.append(valid_now)
    send_list = jnp.stack(list_parts, axis=0)
    send_valid = jnp.stack(valid_parts, axis=0)
    context = (
        own_cols,
        own_global,
        send_list,
        send_valid,
        columns,
        grid_pos,
        grid_size,
        panel_len,
        distances,
    )
    current = blocks
    for turn in range(STEPS):
        square = pattern_product(current, current, context).astype(jnp.bfloat16)
        cube = pattern_product(current, square, context)
        current = (1.5 * current.astype(jnp.float32) - 0.5 * cube).astype(jnp.bfloat16)
    return current


GRID = 4
LAYER = 4
MESH = pl.DeviceIdType.MESH


class Exchange:
    def __init__(self, held, ways, send, recv, place):
        self.held, self.send, self.recv, self.place = held, send, recv, place
        self.ways = [way for way, _ in ways]
        self.sizes = [size for _, size in ways]
        self.starts = [sum(self.sizes[:piece]) for piece in range(len(ways))]
        self.started = []

    def part(self, side, layer, piece):
        start = (side * LAYER + layer) * sum(self.sizes) + self.starts[piece]
        return self.held.at[pl.ds(start, self.sizes[piece])]

    def copy(self, source, stage, side, layer, piece, target):
        return pltpu.make_async_remote_copy(
            src_ref=source,
            dst_ref=self.part(side, layer, piece),
            send_sem=self.send.at[stage, side, piece],
            recv_sem=self.recv.at[stage, side, piece],
            device_id=target,
            device_id_type=MESH,
        )

    def start(self, source, stage, side, layer, piece, target):
        copy = self.copy(source, stage, side, layer, piece, target)
        copy.start()
        self.started.append(copy)

    def arrive(self, stage, side, layer, piece):
        part = self.part(side, layer, piece)
        self.copy(part, stage, side, layer, piece, {"layer": self.place.sibling}).wait_recv()

    def begin(self, source, pieces=None):
        at = self.place
        for piece in range(len(self.ways)) if pieces is None else pieces:
            for side in (1 - at.far, at.far):
                panel = at.panel(side)
                mine = source(side, pl.ds(self.starts[piece], self.sizes[piece]))
                self.start(mine, 0, 1 - side, at.layer, piece, {"grid": panel})
                if self.ways[piece] == "direct":
                    target = {"grid": panel, "layer": at.across}
                    self.start(mine, 2, 1 - side, at.layer, piece, target)

    def spread(self, pieces=None):
        at = self.place
        for piece in range(len(self.ways)) if pieces is None else pieces:
            for side in (1 - at.far, at.far):
                self.arrive(0, side, at.layer, piece)
                part = self.part(side, at.layer, piece)
                if self.ways[piece] != "direct":
                    self.start(part, 2, side, at.layer, piece, {"layer": at.across})
                if self.ways[piece] == "both":
                    self.start(part, 3, side, at.layer, piece, {"layer": at.opposite})
                self.start(part, 1, side, at.layer, piece, {"layer": at.sibling})

    def relay(self):
        at = self.place
        for piece, way in enumerate(self.ways):
            for side in (1 - at.far, at.far):
                if way != "both":
                    self.arrive(2, side, at.across, piece)
                    part = self.part(side, at.across, piece)
                    self.start(part, 3, side, at.across, piece, {"layer": at.sibling})

    def finish(self):
        at = self.place
        for piece, way in enumerate(self.ways):
            for side in (1 - at.far, at.far):
                if way == "both":
                    self.arrive(2, side, at.across, piece)
                self.arrive(1, side, at.sibling, piece)
                self.arrive(3, side, at.opposite, piece)

    def drain(self):
        for copy in self.started:
            copy.wait_send()


class Place:
    def __init__(self):
        self.grid = lax.axis_index("grid")
        self.layer = lax.axis_index("layer")
        self.sibling = self.layer + 1 - 2 * lax.rem(self.layer, 2)
        self.across = lax.rem(self.layer + 2, LAYER)
        self.opposite = lax.rem(self.sibling + 2, LAYER)
        self.far = 1 - self.grid // (GRID - 1)

    def panel(self, side):
        return lax.rem(self.grid + 1 + (GRID - 2) * side, GRID)


def calm(count):
    return [("relay", 1)] * count


def urgent(count):
    return [("relay", 1)] * (count - 1) + [("direct", 1)]


def mutual_ways(count):
    return [("relay", 1)] * (count - 1) + [("direct", 1)]


def dot(left, right):
    return jnp.dot(left, right, preferred_element_type=jnp.float32)


def kernel(
    rows,
    slots,
    cap,
    cols_in,
    x_in,
    out,
    cols,
    x,
    pack,
    mutual,
    diag,
    sq_diag,
    diag1,
    sq_diag1,
    own_sq,
    own_diag1,
    own_sq1,
    sq,
    sq_mut,
    x1,
    x1_mut,
    send_m,
    recv_m,
    send_d,
    recv_d,
    load_sem,
):
    place = Place()
    panel = rows * LAYER
    first = (place.grid * LAYER + place.layer) * rows
    width = x.shape[-1]
    factor = (2.0 * width) ** (-0.5)
    kept = [(a, t) for a in range(rows) for t in range(1, slots)]

    barrier = pltpu.get_barrier_semaphore()
    before, after = {"grid": place.panel(1)}, {"grid": place.panel(0)}
    across = {"layer": place.across}
    partners = [before, after, before | across, after | across, across]
    partners += [{"layer": place.sibling}, {"layer": place.opposite}]
    for target in partners:
        pl.semaphore_signal(barrier, inc=1, device_id=target, device_id_type=MESH)
    loads = [
        pltpu.make_async_copy(cols_in, cols, load_sem.at[0]),
        pltpu.make_async_copy(x_in, x, load_sem.at[1]),
    ]
    for load in loads:
        load.start()
    for load in loads:
        load.wait()

    own_cols = {(a, t): cols[t, first + a] for a, t in kept}
    ahead = {
        key: ((col // panel) == place.panel(0)).astype(jnp.int32) for key, col in own_cols.items()
    }
    for side in range(2):
        source_row = [jnp.int32(0)] * cap
        source_slot = [jnp.int32(1)] * cap
        rank = jnp.int32(0)
        for a, t in kept:
            here = ahead[a, t] if side == 0 else 1 - ahead[a, t]
            for k in range(cap):
                taken = (here == 1) & (rank == k)
                source_row[k] = jnp.where(taken, a, source_row[k])
                source_slot[k] = jnp.where(taken, t, source_slot[k])
            rank = rank + here
        for k in range(cap):
            pack[side, k] = x[source_row[k], source_slot[k]]
    nothing = 2 * LAYER * cap
    mutual[nothing] = jnp.zeros((width, width), jnp.bfloat16)

    pl.semaphore_wait(barrier, len(partners))

    m_trade = Exchange(mutual, mutual_ways(cap), send_m, recv_m, place)
    d_trade, s_trade, d1_trade, s1_trade = [
        Exchange(held, ways(rows), send_d.at[which], recv_d.at[which], place)
        for which, (held, ways) in enumerate(
            ((diag, calm), (sq_diag, urgent), (diag1, calm), (sq_diag1, urgent))
        )
    ]
    m_trade.begin(lambda side, blocks: pack.at[side, blocks])
    d_trade.begin(lambda side, blocks: x.at[blocks, 0])

    at_diag = {}
    at_mutual = {}
    for a, t in kept:
        col = own_cols[a, t]
        side = 1 - ahead[a, t]
        inner = lax.rem(col, panel)
        owner = inner // rows
        within = lax.rem(inner, rows)
        start = col - within
        at_diag[a, t] = (side * LAYER + owner) * rows + within
        found = jnp.int32(nothing)
        rank = jnp.int32(0)
        for b, u in kept:
            theirs = cols[u, start + b]
            hit = (within == b) & (theirs == first + a)
            found = jnp.where(hit, (side * LAYER + owner) * cap + rank, found)
            rank = rank + (theirs // panel == place.grid).astype(jnp.int32)
        at_mutual[a, t] = found

    def row_dot(left, right):
        return dot(jnp.concatenate(left, axis=1), jnp.concatenate(right, axis=0))

    def rounded(product):
        return (product * factor).astype(jnp.bfloat16)

    def stepped(old, product):
        return (1.5 * old.astype(jnp.float32) - 0.5 * (product * factor)).astype(jnp.bfloat16)

    m_trade.spread()
    m_trade.relay()
    m_trade.finish()

    for a in range(rows):
        met = [x[a, 0]] + [mutual[at_mutual[a, t]] for t in range(1, slots)]
        own_sq[a] = rounded(row_dot([x[a, t] for t in range(slots)], met))
    s_trade.begin(lambda side, blocks: own_sq.at[blocks])

    d_trade.spread()
    m_trade.drain()
    s_trade.spread([0])
    d_trade.relay()
    d_trade.finish()

    for a, t in kept:
        theirs, theirs_diag = mutual[at_mutual[a, t]], diag[at_diag[a, t]]
        sq_mut[a, t - 1] = rounded(row_dot([theirs_diag, theirs], [theirs, x[a, 0]]))
    for a in range(rows):
        met = [own_sq[a]] + [sq_mut[a, t - 1] for t in range(1, slots)]
        own_diag1[a] = stepped(x[a, 0], row_dot([x[a, t] for t in range(slots)], met))
    d1_trade.begin(lambda side, blocks: own_diag1.at[blocks])

    s_trade.spread(range(1, len(s_trade.ways)))
    for a, t in kept:
        sq[a, t - 1] = rounded(row_dot([x[a, 0], x[a, t]], [x[a, t], diag[at_diag[a, t]]]))
    s_trade.relay()
    for a, t in kept:
        theirs, theirs_diag = mutual[at_mutual[a, t]], diag[at_diag[a, t]]
        x1_mut[a, t - 1] = stepped(
            theirs, row_dot([theirs_diag, theirs], [sq_mut[a, t - 1], own_sq[a]])
        )
    s_trade.finish()

    for a, t in kept:
        x1[a, t - 1] = stepped(
            x[a, t], row_dot([x[a, 0], x[a, t]], [sq[a, t - 1], sq_diag[at_diag[a, t]]])
        )
    for a in range(rows):
        left = [own_diag1[a]] + [x1[a, t - 1] for t in range(1, slots)]
        right = [own_diag1[a]] + [x1_mut[a, t - 1] for t in range(1, slots)]
        own_sq1[a] = rounded(row_dot(left, right))
    s1_trade.begin(lambda side, blocks: own_sq1.at[blocks])

    d_trade.drain()
    s_trade.drain()
    d1_trade.spread()
    s1_trade.spread([0])
    d1_trade.relay()
    d1_trade.finish()

    for a, t in kept:
        theirs, theirs_diag = x1_mut[a, t - 1], diag1[at_diag[a, t]]
        sq_mut[a, t - 1] = rounded(row_dot([theirs_diag, theirs], [theirs, own_diag1[a]]))
        sq[a, t - 1] = rounded(
            row_dot([own_diag1[a], x1[a, t - 1]], [x1[a, t - 1], theirs_diag])
        )
    s1_trade.spread(range(1, len(s1_trade.ways)))
    s1_trade.relay()
    for a in range(rows):
        left = [own_diag1[a]] + [x1[a, t - 1] for t in range(1, slots)]
        met = [own_sq1[a]] + [sq_mut[a, t - 1] for t in range(1, slots)]
        out[a, 0] = stepped(own_diag1[a], row_dot(left, met))
    d1_trade.drain()
    s1_trade.finish()
    for a, t in kept:
        out[a, t] = stepped(
            x1[a, t - 1],
            row_dot([own_diag1[a], x1[a, t - 1]], [sq[a, t - 1], sq_diag1[at_diag[a, t]]]),
        )
    s1_trade.drain()


def local_kernel(blocks, columns):
    rows, slots, width, _ = blocks.shape
    moved = rows * (slots - 1)
    cap = 2 * ((moved + 3) // 4)

    def held(*dims):
        return pltpu.VMEM(dims + (width, width), jnp.bfloat16)

    beside = 2 * LAYER * rows
    m_sems = (4, 2, cap)
    d_sems = (4, 4, 2, rows)
    return pl.pallas_call(
        functools.partial(kernel, rows, slots, cap),
        out_shape=jax.ShapeDtypeStruct(blocks.shape, blocks.dtype),
        in_specs=[
            pl.BlockSpec(memory_space=pltpu.HBM),
            pl.BlockSpec(memory_space=pltpu.HBM),
        ],
        out_specs=pl.BlockSpec(memory_space=pltpu.VMEM),
        scratch_shapes=[
            pltpu.SMEM(columns.shape[::-1], columns.dtype),
            pltpu.VMEM(blocks.shape, blocks.dtype),
            held(2, cap),
            held(2 * LAYER * cap + 1),
            held(beside),
            held(beside),
            held(beside),
            held(beside),
            held(rows),
            held(rows),
            held(rows),
            held(rows, slots - 1),
            held(rows, slots - 1),
            held(rows, slots - 1),
            held(rows, slots - 1),
            pltpu.SemaphoreType.DMA(m_sems),
            pltpu.SemaphoreType.DMA(m_sems),
            pltpu.SemaphoreType.DMA(d_sems),
            pltpu.SemaphoreType.DMA(d_sems),
            pltpu.SemaphoreType.DMA((2,)),
        ],
        compiler_params=pltpu.CompilerParams(
            collective_id=0, has_side_effects=True, vmem_limit_bytes=64 * 1024 * 1024
        ),
        name="sign_iterations",
    )(columns.T, blocks)


def solution(mesh):
    placed = (P(("groups", "grid", "layer"), None, None, None), P("groups", None))
    four_panels = mesh.shape["grid"] == GRID and mesh.shape["layer"] == LAYER
    return jax.shard_map(
        local_kernel if four_panels else local,
        mesh=mesh,
        in_specs=placed,
        out_specs=P(("groups", "grid", "layer"), None, None, None),
        check_vma=False,
    )
```

```python
import functools

import jax
import jax.numpy as jnp
from jax import lax
from jax.experimental import pallas as pl
from jax.experimental.pallas import tpu as pltpu
from jax.sharding import PartitionSpec as P

STEPS = 2


def from_behind(block, axis, distance):
    devices = range(lax.axis_size(axis))
    route = [((i - distance) % len(devices), i) for i in devices]
    return lax.ppermute(block, axis, route)


def pattern_product(multiplier, operand, context):
    (
        own_cols,
        own_global,
        send_list,
        send_valid,
        columns,
        grid_pos,
        grid_size,
        panel_len,
        distances,
    ) = context
    rows_own = multiplier.shape[0]
    slots = multiplier.shape[1]
    width = multiplier.shape[2]
    flat_list = send_list.reshape(-1)
    flat_valid = send_valid.reshape(-1)
    piece = lax.all_gather(operand, "layer", axis=0, tiled=True)
    picker = (
        (flat_list[:, None] == jnp.arange(piece.shape[0])[None, :]) & flat_valid[:, None]
    ).astype(jnp.bfloat16)
    chosen = jnp.einsum("rn,nuij->ruij", picker, piece, preferred_element_type=jnp.float32)
    packed = chosen.astype(jnp.bfloat16)
    packed = packed.reshape(send_list.shape + (slots, width, width))
    arrived = []
    for kind in range(len(distances)):
        arrived.append(from_behind((packed[kind], send_list[kind]), "grid", -distances[kind]))
    cand_blocks = jnp.concatenate([operand] + [entry[0] for entry in arrived], axis=0)
    cand_parts = [own_global]
    for kind in range(len(distances)):
        source = (grid_pos + distances[kind]) % grid_size
        cand_parts.append(source * panel_len + arrived[kind][1])
    cand_rows = jnp.concatenate(cand_parts, axis=0).astype(jnp.int32)
    cand_cols = jnp.take(columns, cand_rows, axis=0)
    wanted = own_cols.reshape(-1)
    matches = wanted[:, None] == cand_rows[None, :]
    gathered = jnp.einsum(
        "ac,cuij->auij",
        matches.astype(jnp.bfloat16),
        cand_blocks,
        preferred_element_type=jnp.float32,
    ).astype(jnp.bfloat16)
    gathered_cols = jnp.max(jnp.where(matches[:, :, None], cand_cols[None, :, :], -1), axis=1)
    partial_value = jnp.einsum(
        "aij,aujk->auik",
        multiplier.reshape(-1, width, width),
        gathered,
        preferred_element_type=jnp.float32,
    )
    agree = (
        gathered_cols.reshape(rows_own, slots, slots)[:, :, :, None] == own_cols[:, None, None, :]
    ).astype(jnp.float32)
    summed = jnp.einsum(
        "qtus,qtuik->qsik",
        agree,
        partial_value.reshape(rows_own, slots, slots, width, width),
        precision=lax.Precision.HIGHEST,
    )
    return summed * (2.0 * width) ** (-0.5)


def local(blocks, columns):
    rows_own = blocks.shape[0]
    slots = blocks.shape[1]
    grid_size = lax.axis_size("grid")
    layer_size = lax.axis_size("layer")
    panel_len = rows_own * layer_size
    grid_pos = lax.axis_index("grid")
    layer_pos = lax.axis_index("layer")
    first_row = (grid_pos * layer_size + layer_pos) * rows_own
    own_global = first_row + jnp.arange(rows_own)
    own_cols = lax.dynamic_slice_in_dim(columns, first_row, rows_own, 0)
    reach = min(3, (grid_size - 1) // 2)
    moved_slots = rows_own * (slots - 1)
    pack_len = 2 * ((moved_slots + 4 * reach - 1) // (4 * reach))
    distances = [offset + 1 for offset in range(reach)] + [-(offset + 1) for offset in range(reach)]
    slot_index = jnp.arange(moved_slots, dtype=jnp.int32)
    position = jnp.arange(pack_len, dtype=jnp.int32)
    list_parts = []
    valid_parts = []
    for shift_by in distances:
        source_grid = (grid_pos - shift_by) % grid_size
        source_start = (source_grid * layer_size + layer_pos) * rows_own
        source_cols = lax.dynamic_slice_in_dim(columns, source_start, rows_own, 0)[:, 1:].reshape(
            -1
        )
        matched = source_cols // panel_len == grid_pos
        ordering = jnp.argsort(jnp.where(matched, 0, moved_slots) + slot_index)[:pack_len]
        local_rows = source_cols[ordering] - grid_pos * panel_len
        counted = jnp.sum(matched.astype(jnp.int32))
        valid_now = position < counted
        list_parts.append(jnp.where(valid_now, local_rows, 0))
        valid_parts.append(valid_now)
    send_list = jnp.stack(list_parts, axis=0)
    send_valid = jnp.stack(valid_parts, axis=0)
    context = (
        own_cols,
        own_global,
        send_list,
        send_valid,
        columns,
        grid_pos,
        grid_size,
        panel_len,
        distances,
    )
    current = blocks
    for turn in range(STEPS):
        square = pattern_product(current, current, context).astype(jnp.bfloat16)
        cube = pattern_product(current, square, context)
        current = (1.5 * current.astype(jnp.float32) - 0.5 * cube).astype(jnp.bfloat16)
    return current


GRID = 4
LAYER = 4
MESH = pl.DeviceIdType.MESH


class Exchange:
    def __init__(self, held, ways, send, recv, place):
        self.held, self.send, self.recv, self.place = held, send, recv, place
        self.ways = [way for way, _ in ways]
        self.sizes = [size for _, size in ways]
        self.starts = [sum(self.sizes[:piece]) for piece in range(len(ways))]
        self.started = []

    def part(self, side, layer, piece):
        start = (side * LAYER + layer) * sum(self.sizes) + self.starts[piece]
        return self.held.at[pl.ds(start, self.sizes[piece])]

    def copy(self, source, stage, side, layer, piece, target):
        return pltpu.make_async_remote_copy(
            src_ref=source,
            dst_ref=self.part(side, layer, piece),
            send_sem=self.send.at[stage, side, piece],
            recv_sem=self.recv.at[stage, side, piece],
            device_id=target,
            device_id_type=MESH,
        )

    def start(self, source, stage, side, layer, piece, target):
        copy = self.copy(source, stage, side, layer, piece, target)
        copy.start()
        self.started.append(copy)

    def arrive(self, stage, side, layer, piece):
        part = self.part(side, layer, piece)
        self.copy(part, stage, side, layer, piece, {"layer": self.place.sibling}).wait_recv()

    def begin(self, source, pieces=None):
        at = self.place
        for piece in range(len(self.ways)) if pieces is None else pieces:
            for side in (1 - at.far, at.far):
                panel = at.panel(side)
                mine = source(side, pl.ds(self.starts[piece], self.sizes[piece]))
                self.start(mine, 0, 1 - side, at.layer, piece, {"grid": panel})
                if self.ways[piece] == "direct":
                    target = {"grid": panel, "layer": at.across}
                    self.start(mine, 2, 1 - side, at.layer, piece, target)

    def spread(self, pieces=None):
        at = self.place
        for piece in range(len(self.ways)) if pieces is None else pieces:
            for side in (1 - at.far, at.far):
                self.arrive(0, side, at.layer, piece)
                part = self.part(side, at.layer, piece)
                if self.ways[piece] != "direct":
                    self.start(part, 2, side, at.layer, piece, {"layer": at.across})
                if self.ways[piece] == "both":
                    self.start(part, 3, side, at.layer, piece, {"layer": at.opposite})
                self.start(part, 1, side, at.layer, piece, {"layer": at.sibling})

    def relay(self, pieces=None):
        at = self.place
        for piece in range(len(self.ways)) if pieces is None else pieces:
            way = self.ways[piece]
            for side in (1 - at.far, at.far):
                if way != "both":
                    self.arrive(2, side, at.across, piece)
                    part = self.part(side, at.across, piece)
                    self.start(part, 3, side, at.across, piece, {"layer": at.sibling})

    def finish(self):
        at = self.place
        for piece, way in enumerate(self.ways):
            for side in (1 - at.far, at.far):
                if way == "both":
                    self.arrive(2, side, at.across, piece)
                self.arrive(1, side, at.sibling, piece)
                self.arrive(3, side, at.opposite, piece)

    def drain(self):
        for copy in self.started:
            copy.wait_send()


class Place:
    def __init__(self):
        self.grid = lax.axis_index("grid")
        self.layer = lax.axis_index("layer")
        self.sibling = self.layer + 1 - 2 * lax.rem(self.layer, 2)
        self.across = lax.rem(self.layer + 2, LAYER)
        self.opposite = lax.rem(self.sibling + 2, LAYER)
        self.far = 1 - self.grid // (GRID - 1)

    def panel(self, side):
        return lax.rem(self.grid + 1 + (GRID - 2) * side, GRID)


def calm(count):
    return [("relay", 1)] * count


def urgent(count):
    return [("relay", 1)] * (count - 1) + [("direct", 1)]


def mutual_ways(count):
    return [("relay", 1)] * (count - 1) + [("direct", 1)]


def dot(left, right):
    return jnp.dot(left, right, preferred_element_type=jnp.float32)


def kernel(
    rows,
    slots,
    cap,
    cols_in,
    x_in,
    out,
    cols,
    x,
    pack,
    mutual,
    diag,
    sq_diag,
    diag1,
    sq_diag1,
    own_sq,
    own_diag1,
    own_sq1,
    sq,
    sq_mut,
    x1,
    x1_mut,
    send_m,
    recv_m,
    send_d,
    recv_d,
    load_sem,
):
    place = Place()
    panel = rows * LAYER
    first = (place.grid * LAYER + place.layer) * rows
    width = x.shape[-1]
    factor = (2.0 * width) ** (-0.5)
    kept = [(a, t) for a in range(rows) for t in range(1, slots)]

    barrier = pltpu.get_barrier_semaphore()
    before, after = {"grid": place.panel(1)}, {"grid": place.panel(0)}
    across = {"layer": place.across}
    partners = [before, after, before | across, after | across, across]
    partners += [{"layer": place.sibling}]
    for target in partners:
        pl.semaphore_signal(barrier, inc=1, device_id=target, device_id_type=MESH)
    loads = [
        pltpu.make_async_copy(cols_in, cols, load_sem.at[0]),
        pltpu.make_async_copy(x_in, x, load_sem.at[1]),
    ]
    for load in loads:
        load.start()
    for load in loads:
        load.wait()

    own_cols = {(a, t): cols[t, first + a] for a, t in kept}
    ahead = {
        key: ((col // panel) == place.panel(0)).astype(jnp.int32) for key, col in own_cols.items()
    }
    for side in range(2):
        source_row = [jnp.int32(0)] * cap
        source_slot = [jnp.int32(1)] * cap
        rank = jnp.int32(0)
        for a, t in kept:
            here = ahead[a, t] if side == 0 else 1 - ahead[a, t]
            for k in range(cap):
                taken = (here == 1) & (rank == k)
                source_row[k] = jnp.where(taken, a, source_row[k])
                source_slot[k] = jnp.where(taken, t, source_slot[k])
            rank = rank + here
        for k in range(cap):
            pack[side, k] = x[source_row[k], source_slot[k]]
    nothing = 2 * LAYER * cap
    mutual[nothing] = jnp.zeros((width, width), jnp.bfloat16)

    pl.semaphore_wait(barrier, len(partners))

    m_trade = Exchange(mutual, mutual_ways(cap), send_m, recv_m, place)
    d_trade, s_trade, d1_trade, s1_trade = [
        Exchange(held, ways(rows), send_d.at[which], recv_d.at[which], place)
        for which, (held, ways) in enumerate(
            ((diag, calm), (sq_diag, urgent), (diag1, calm), (sq_diag1, urgent))
        )
    ]
    m_trade.begin(lambda side, blocks: pack.at[side, blocks])
    d_trade.begin(lambda side, blocks: x.at[blocks, 0])

    at_diag = {}
    at_mutual = {}
    for a, t in kept:
        col = own_cols[a, t]
        side = 1 - ahead[a, t]
        inner = lax.rem(col, panel)
        owner = inner // rows
        within = lax.rem(inner, rows)
        start = col - within
        at_diag[a, t] = (side * LAYER + owner) * rows + within
        found = jnp.int32(nothing)
        rank = jnp.int32(0)
        for b, u in kept:
            theirs = cols[u, start + b]
            hit = (within == b) & (theirs == first + a)
            found = jnp.where(hit, (side * LAYER + owner) * cap + rank, found)
            rank = rank + (theirs // panel == place.grid).astype(jnp.int32)
        at_mutual[a, t] = found

    def row_dot(left, right):
        return dot(jnp.concatenate(left, axis=1), jnp.concatenate(right, axis=0))

    def rounded(product):
        return (product * factor).astype(jnp.bfloat16)

    def stepped(old, product):
        return (1.5 * old.astype(jnp.float32) - 0.5 * (product * factor)).astype(jnp.bfloat16)

    m_trade.spread(range(cap - 1))
    m_trade.relay([0])
    m_trade.spread([cap - 1])
    m_trade.relay(range(1, cap))
    m_trade.finish()

    for a in range(rows):
        met = [x[a, 0]] + [mutual[at_mutual[a, t]] for t in range(1, slots)]
        own_sq[a] = rounded(row_dot([x[a, t] for t in range(slots)], met))
    s_trade.begin(lambda side, blocks: own_sq.at[blocks])

    d_trade.spread()
    m_trade.drain()
    s_trade.spread([0])
    d_trade.relay()
    d_trade.finish()

    for a, t in kept:
        theirs, theirs_diag = mutual[at_mutual[a, t]], diag[at_diag[a, t]]
        sq_mut[a, t - 1] = rounded(row_dot([theirs_diag, theirs], [theirs, x[a, 0]]))
    for a in range(rows):
        met = [own_sq[a]] + [sq_mut[a, t - 1] for t in range(1, slots)]
        own_diag1[a] = stepped(x[a, 0], row_dot([x[a, t] for t in range(slots)], met))
    d1_trade.begin(lambda side, blocks: own_diag1.at[blocks])

    s_trade.spread(range(1, len(s_trade.ways)))
    for a, t in kept:
        sq[a, t - 1] = rounded(row_dot([x[a, 0], x[a, t]], [x[a, t], diag[at_diag[a, t]]]))
    s_trade.relay()
    for a, t in kept:
        theirs, theirs_diag = mutual[at_mutual[a, t]], diag[at_diag[a, t]]
        x1_mut[a, t - 1] = stepped(
            theirs, row_dot([theirs_diag, theirs], [sq_mut[a, t - 1], own_sq[a]])
        )
    s_trade.finish()

    for a, t in kept:
        x1[a, t - 1] = stepped(
            x[a, t], row_dot([x[a, 0], x[a, t]], [sq[a, t - 1], sq_diag[at_diag[a, t]]])
        )
    for a in range(rows):
        left = [own_diag1[a]] + [x1[a, t - 1] for t in range(1, slots)]
        right = [own_diag1[a]] + [x1_mut[a, t - 1] for t in range(1, slots)]
        own_sq1[a] = rounded(row_dot(left, right))
    s1_trade.begin(lambda side, blocks: own_sq1.at[blocks])

    d_trade.drain()
    s_trade.drain()
    d1_trade.spread()
    s1_trade.spread([0])
    d1_trade.relay()
    d1_trade.finish()

    for a, t in kept:
        theirs, theirs_diag = x1_mut[a, t - 1], diag1[at_diag[a, t]]
        sq_mut[a, t - 1] = rounded(row_dot([theirs_diag, theirs], [theirs, own_diag1[a]]))
        sq[a, t - 1] = rounded(
            row_dot([own_diag1[a], x1[a, t - 1]], [x1[a, t - 1], theirs_diag])
        )
    s1_trade.spread(range(1, len(s1_trade.ways)))
    s1_trade.relay()
    for a in range(rows):
        left = [own_diag1[a]] + [x1[a, t - 1] for t in range(1, slots)]
        met = [own_sq1[a]] + [sq_mut[a, t - 1] for t in range(1, slots)]
        out[a, 0] = stepped(own_diag1[a], row_dot(left, met))
    d1_trade.drain()
    s1_trade.finish()
    for a, t in kept:
        out[a, t] = stepped(
            x1[a, t - 1],
            row_dot([own_diag1[a], x1[a, t - 1]], [sq[a, t - 1], sq_diag1[at_diag[a, t]]]),
        )
    s1_trade.drain()


def local_kernel(blocks, columns):
    rows, slots, width, _ = blocks.shape
    moved = rows * (slots - 1)
    cap = 2 * ((moved + 3) // 4)

    def held(*dims):
        return pltpu.VMEM(dims + (width, width), jnp.bfloat16)

    beside = 2 * LAYER * rows
    m_sems = (4, 2, cap)
    d_sems = (4, 4, 2, rows)
    return pl.pallas_call(
        functools.partial(kernel, rows, slots, cap),
        out_shape=jax.ShapeDtypeStruct(blocks.shape, blocks.dtype),
        in_specs=[
            pl.BlockSpec(memory_space=pltpu.HBM),
            pl.BlockSpec(memory_space=pltpu.HBM),
        ],
        out_specs=pl.BlockSpec(memory_space=pltpu.VMEM),
        scratch_shapes=[
            pltpu.SMEM(columns.shape[::-1], columns.dtype),
            pltpu.VMEM(blocks.shape, blocks.dtype),
            held(2, cap),
            held(2 * LAYER * cap + 1),
            held(beside),
            held(beside),
            held(beside),
            held(beside),
            held(rows),
            held(rows),
            held(rows),
            held(rows, slots - 1),
            held(rows, slots - 1),
            held(rows, slots - 1),
            held(rows, slots - 1),
            pltpu.SemaphoreType.DMA(m_sems),
            pltpu.SemaphoreType.DMA(m_sems),
            pltpu.SemaphoreType.DMA(d_sems),
            pltpu.SemaphoreType.DMA(d_sems),
            pltpu.SemaphoreType.DMA((2,)),
        ],
        compiler_params=pltpu.CompilerParams(
            collective_id=0, has_side_effects=True, vmem_limit_bytes=64 * 1024 * 1024
        ),
        name="sign_iterations",
    )(columns.T, blocks)


def solution(mesh):
    placed = (P(("groups", "grid", "layer"), None, None, None), P("groups", None))
    four_panels = mesh.shape["grid"] == GRID and mesh.shape["layer"] == LAYER
    return jax.shard_map(
        local_kernel if four_panels else local,
        mesh=mesh,
        in_specs=placed,
        out_specs=P(("groups", "grid", "layer"), None, None, None),
        check_vma=False,
    )
```
